512 devices in a mesh: bead: 8 (over z_hi, x), space: 64 (over y, z_lo, core).
Axes of the slice: x: 4, y: 8, z: 8 (z_hi: 2, z_lo: 4; z = z_hi * 4 + z_lo), core: 2. Of those that a mesh axis runs over, the one named last changes fastest.
Arguments:
- positions: float32 [32, 3, 24576], P('bead', None, 'space'), as said below
- charges: float32 [24576], P('space'), may hold values from -3 to 3
- polar: float32 [24576], P('space'), may hold values from 0.4 to 1.6
- molecule: int32 [24576], P('space'), may hold values from 0 to 8191, as said below
Outputs:
- total_field: float32 [32, 3, 24576], P('bead', None, 'space')
- dipoles: float32 [4, 3, 24576], P(None, None, 'space')
The draws below stay inside these ranges and needn't reach their ends.
Inputs may be any that keep to these rules, and one draw needn't show every extreme that they name: Each molecule has three atoms, all in one slab block of 384 atoms; no id appears in two blocks. `positions`: in slab block d every atom's first coordinate lies between 15.2 d and 15.2 (d + 1).
All inputs are finite; a program needn't handle non-finite values.
Results may differ from the reference program's by a relative error of at most 0.0003.
Values sent between devices are 32-bit elements; how exact they have to be, the bound alone decides.
A program may use at most 64 MiB of HBM per device.

```python
import math
import jax
import jax.numpy as jnp
from jax import lax

BEADS = 32
CONTR = 4
ITERS = 2
ROWS_Y = 4
ATOMS_DEV = 384
ATOMS = 24576


def atom_roles(key):
    domains = ATOMS // ATOMS_DEV
    keys = jax.random.split(jax.random.fold_in(key, 11), domains)
    return jax.vmap(lambda k: jax.random.permutation(k, ATOMS_DEV))(keys).astype(jnp.int32)


def draw_molecule(key, part):
    roles = atom_roles(key)
    domains = roles.shape[0]
    base = jnp.arange(domains, dtype=jnp.int32)[:, None] * (ATOMS_DEV // 3)
    return (base + roles // 3).reshape(-1)


def draw_positions(key, part):
    roles = atom_roles(key)
    domains = roles.shape[0]
    mols = ATOMS_DEV // 3
    spacing = 3.8
    mol = roles // 3
    kind = roles % 3
    first, second, third = jax.random.split(jax.random.fold_in(key, 23), 3)
    jitter = jax.random.uniform(first, (domains, mols, 3), jnp.float32, -0.3, 0.3)
    arms = jax.random.normal(second, (domains, mols * 2, 3), jnp.float32)
    arms = arms / jnp.sqrt(jnp.sum(arms * arms, axis=-1, keepdims=True) + 1e-12)
    xrow = (mol % 4).astype(jnp.float32)
    yrow = (mol // 4 % ROWS_Y).astype(jnp.float32)
    zrow = (mol // (4 * ROWS_Y)).astype(jnp.float32)
    slab = jnp.arange(domains, dtype=jnp.float32)[:, None] * 4.0 * spacing
    centre = jnp.stack([slab + (xrow + 0.5) * spacing, (yrow + 0.5) * spacing, (zrow + 0.5) * spacing], -1)
    centre = centre + jnp.take_along_axis(jitter, jnp.broadcast_to(mol[:, :, None], (domains, ATOMS_DEV, 3)), axis=1)
    which = mol * 2 + jnp.maximum(kind - 1, 0)
    chosen = jnp.take_along_axis(arms, jnp.broadcast_to(which[:, :, None], (domains, ATOMS_DEV, 3)), axis=1)
    atom = centre + jnp.where((kind > 0)[:, :, None], 0.96 * chosen, 0.0)
    atom = atom.reshape(domains * ATOMS_DEV, 3).T
    offsets = jnp.clip(0.1 * jax.random.normal(third, (BEADS, 3, ATOMS), jnp.float32), -0.3, 0.3)
    return atom[None] + offsets


def steps_of(own_key, dims, pieces, low, largest):
    def one(position, shards_of):
        draws = jax.random.uniform(jax.random.fold_in(jax.random.fold_in(own_key, 6), position), (shards_of,), jnp.float32, low / len(pieces), largest / len(pieces))
        return jnp.repeat(jnp.exp(draws), dims[position] // shards_of).reshape((-1,) + (1,) * (len(dims) - position - 1))

    level = one(*pieces[0])
    for cut in pieces[1:]:
        level = level * one(*cut)
    return level


def gaussian(key, shape, deviation, limit, cuts=(), kind=jnp.bfloat16):
    values = jax.random.normal(key, shape, jnp.float32) * deviation
    if len(cuts) > 0:
        values = steps_of(key, shape, cuts, -0.22, 0.18) * values
    return jnp.clip(values, min=-limit, max=limit).astype(kind)


def setup_inputs(seed: int = 0) -> dict:
    arg_keys = jax.random.split(jax.random.key(seed), 5)
    return {
        "positions": draw_positions(jax.random.fold_in(arg_keys[4], 71), 0),
        "charges": gaussian(arg_keys[1], (ATOMS,), 0.5, 3.0, ((0, 64),), jnp.float32),
        "polar": jnp.clip(jnp.exp(math.log(1.6) - 1.3862944 * jax.random.uniform(arg_keys[2], (ATOMS,), jnp.float32) ** steps_of(arg_keys[2], (ATOMS,), ((0, 64),), -0.2, 0.2)), 0.4, 1.6),
        "molecule": draw_molecule(jax.random.fold_in(arg_keys[4], 71), 0),
    }


THOLE = 0.39
CUTOFF = 9.0

def pair_field(target, target_alpha, target_mol, source, source_charge, source_alpha, source_dip, source_mol, dipolar):
    width = source.shape[1] // 18
    count = source.shape[1] // width
    blocks = (source.reshape(3, count, width).transpose(1, 0, 2), source_charge.reshape(count, width), source_alpha.reshape(count, width), source_dip.reshape(3, count, width).transpose(1, 0, 2), source_mol.reshape(count, width))

    def step(total, block):
        spot, charge, alpha, dip, mol = block
        diff = target[:, :, None] - spot[:, None, :]
        dist2 = lax.optimization_barrier(jnp.sum(diff * diff, axis=0))
        keep = (alpha[None, :] > 0.0) & (target_mol[:, None] != mol[None, :]) & (dist2 < CUTOFF * CUTOFF)
        safe2 = jnp.where(keep, dist2, 1.0)
        inverse = lax.rsqrt(safe2)
        inv3 = inverse * inverse * inverse
        both = jnp.where(keep, target_alpha[:, None] * alpha[None, :], 1.0)
        cube = 0.39 * safe2 * jnp.sqrt(safe2) * lax.rsqrt(both)
        decay = jnp.exp(-cube)
        damp3 = 1.0 - decay
        damp5 = 1.0 - (1.0 + cube) * decay
        ratio = 1.0 - dist2 / (CUTOFF * CUTOFF)
        taper = jnp.where(keep, ratio * ratio, 0.0)
        if dipolar:
            along = lax.optimization_barrier(jnp.sum(diff * dip[:, None, :], axis=0))
            term = (3.0 * taper * damp5 * inv3 * inverse * inverse * along)[None] * diff - (taper * damp3 * inv3)[None] * dip[:, None, :]
        else:
            term = (taper * damp3 * inv3 * charge[None, :])[None] * diff
        return (total + lax.optimization_barrier(jnp.sum(term, axis=2)), None)
    start = jnp.zeros((3, target.shape[1]), jnp.float32)
    total, unused = lax.scan(step, start, blocks)
    return total

def reference(positions, charges, polar, molecule):
    atoms_dom = ATOMS_DEV
    domains = ATOMS // atoms_dom

    def widen(values, fill):
        edge = jnp.full(values.shape[:-1] + (atoms_dom,), fill, values.dtype)
        return jnp.concatenate([edge, values, edge], -1)
    wide_charge = widen(charges, 0.0)
    wide_alpha = widen(polar, 0.0)
    wide_mol = widen(molecule, -1)

    def field_all(spots, dips, dipolar):
        wide_spots = widen(spots, 0.0)
        wide_dips = widen(dips, 0.0)

        def one(index):
            start = (index * atoms_dom).astype(jnp.int32)
            target = lax.dynamic_slice_in_dim(spots, start, atoms_dom, 1)
            talpha = lax.dynamic_slice_in_dim(polar, start, atoms_dom, 0)
            tmol = lax.dynamic_slice_in_dim(molecule, start, atoms_dom, 0)
            return pair_field(target, talpha, tmol, lax.dynamic_slice_in_dim(wide_spots, start, 3 * atoms_dom, 1), lax.dynamic_slice_in_dim(wide_charge, start, 3 * atoms_dom, 0), lax.dynamic_slice_in_dim(wide_alpha, start, 3 * atoms_dom, 0), lax.dynamic_slice_in_dim(wide_dips, start, 3 * atoms_dom, 1), lax.dynamic_slice_in_dim(wide_mol, start, 3 * atoms_dom, 0), dipolar)
        result = lax.map(one, jnp.arange(domains, dtype=jnp.int32))
        return result.transpose(1, 0, 2).reshape(3, domains * atoms_dom)
    nothing = jnp.zeros((3, ATOMS), jnp.float32)
    perm = lax.map(lambda spots: field_all(spots, nothing, False), positions)
    kidx = jnp.arange(CONTR, dtype=jnp.float32)[:, None] / CONTR
    bidx = jnp.arange(BEADS, dtype=jnp.float32)[None, :] / BEADS
    theta = 2.0 * jnp.pi * (kidx - bidx)
    series = 1.0 + 2.0 * jnp.cos(theta) + jnp.cos(2.0 * theta)
    contract = series / BEADS
    spread = series.T / CONTR
    high = lax.Precision.HIGHEST
    cpos = jnp.einsum('kb,bxa->kxa', contract, positions, precision=high)
    cfield = jnp.einsum('kb,bxa->kxa', contract, perm, precision=high)

    def induce(mu):
        return lax.map(lambda pair: field_all(pair[0], pair[1], True), (cpos, mu))
    mu = polar[None, None, :] * cfield
    for step in range(ITERS):
        mu = polar[None, None, :] * (cfield + induce(mu))
    induced = induce(mu)
    total = perm + jnp.einsum('bk,kxa->bxa', spread, induced, precision=high)
    return (total, mu)
```

```python
import functools
import math

import jax
import jax.numpy as jnp
import numpy as np
from jax import lax
from jax.experimental import pallas as pl
from jax.experimental.pallas import tpu as pltpu
from jax.sharding import PartitionSpec as P

BEADS = 32
CONTR = 4
ITERS = 2
CUT2 = 81.0
MESH = pl.DeviceIdType.MESH
OWN, LEFT, RIGHT = 0, 1, 2


def series(i):
    theta = 2.0 * math.pi * i / BEADS
    return (1.0 + 2.0 * math.cos(theta) + math.cos(2.0 * theta)) / BEADS


def kernel(
    beads, atoms, spaces,
    pos_hbm, charge_hbm, polar_hbm, mol_hbm,
    total_ref, moment_ref,
    pos_ref, charge_ref, polar_ref, mol_ref, in_sem,
    pk, col, perm, cps, cpin, fps, fpin, ctr, ccol, tens, mu, mucol, ind, indin, muin,
    halo_send, halo_recv, cp_send, cp_recv, fp_send, fp_recv, mu_send, mu_recv,
    dip_send, dip_recv, ind_send, ind_recv,
):
    rank = lax.axis_index("bead")
    slab = lax.axis_index("space")
    half, spot = rank // 4, lax.rem(rank, 4)
    left, right = lax.rem(slab + spaces - 1, spaces), lax.rem(slab + 1, spaces)
    row_first, row_last = lax.rem(slab, 8) == 0, lax.rem(slab, 8) == 7
    across = (1 - half) * 4 + spot
    to_left = (rank, left)
    to_right = (rank, right)
    mu_left = (jnp.where(row_first, across, rank), left)
    mu_right = (jnp.where(row_last, across, rank), right)

    slabs = (slab, left, right)

    def peer(turn, dx, side=OWN):
        return ((half if turn == 0 else 1 - half) * 4 + lax.rem(spot + dx, 4), slabs[side])

    others = [(turn, dx) for turn in (1, 0) for dx in (2, 1, 3, 0) if (turn, dx) != (0, 0)]
    around = [(turn, dx, side) for turn in (1, 0) for dx in (2, 1, 3, 0) for side in (LEFT, RIGHT, OWN)]
    around.remove((0, 0, OWN))
    barrier = pltpu.get_barrier_semaphore()
    greeted = [peer(*o) for o in around]
    for device in greeted:
        pl.semaphore_signal(barrier, inc=1, device_id=device, device_id_type=MESH)

    loads = [
        pltpu.make_async_copy(src, dst, in_sem.at[n])
        for n, (src, dst) in enumerate(
            ((pos_hbm, pos_ref), (charge_hbm, charge_ref), (polar_hbm, polar_ref), (mol_hbm, mol_ref))
        )
    ]
    for c in loads:
        c.start()

    def remote(src, dst, send, recv, device):
        return pltpu.make_async_remote_copy(
            src_ref=src, dst_ref=dst, send_sem=send, recv_sem=recv, device_id=device, device_id_type=MESH
        )

    def weight(k, l):
        j = lax.rem(2 * k - rank + 8, 8)
        value = jnp.float32(series(-l))
        for n in range(1, 8):
            value = jnp.where(j == n, jnp.float32(series(4 * n - l)), value)
        return value

    fold = [[weight(lax.rem(spot + dx, 4), l) for l in range(beads)] for dx in range(4)]
    for c in loads:
        c.wait()
    for a in range(3):
        pk[OWN, 4 * a : 4 * a + 4, :] = pos_ref[a]
    alpha = polar_ref[...].reshape(1, atoms)
    root = lax.rsqrt(alpha) * math.sqrt(0.39)
    pk[OWN, 12:13, :] = charge_ref[...].reshape(1, atoms) * (1.0 / (CUT2 * CUT2))
    pk[OWN, 13:14, :] = -root
    pk[OWN, 14:15, :] = mol_ref[...].astype(jnp.float32).reshape(1, atoms)
    pk[OWN, 15:16, :] = alpha

    pl.semaphore_wait(barrier, len(greeted))
    halo = [
        remote(pk.at[OWN], pk.at[RIGHT], halo_send.at[0], halo_recv.at[0], to_left),
        remote(pk.at[OWN], pk.at[LEFT], halo_send.at[1], halo_recv.at[1], to_right),
    ]
    for c in halo:
        c.start()

    def spread(row):
        return jnp.broadcast_to(row, (8, atoms))

    col[OWN] = pk[OWN].T
    gi = spread(root)
    moli = spread(pk[OWN, 14:15, :])
    zero = jnp.zeros((8, atoms), jnp.float32)

    def perm_part(l, side, start):
        target = [spread(pk[OWN, 4 * a + l : 4 * a + l + 1, :]) for a in range(3)]

        def step(i, acc):
            source = col[side, pl.ds(i * 8, 8), :]
            d = [target[a] - source[:, 4 * a + l : 4 * a + l + 1] for a in range(3)]
            r2 = d[0] * d[0] + d[1] * d[1] + d[2] * d[2]
            if side == OWN:
                r2 = jnp.where(moli == source[:, 14:15], CUT2, r2)
            r2 = jnp.minimum(r2, CUT2)
            inv = lax.rsqrt(r2)
            c = (r2 * gi) * source[:, 13:14] * (r2 * inv)
            decay = jnp.exp(c)
            u = (CUT2 - r2) * inv
            w = (u * u) * (inv * source[:, 12:13]) * (1.0 - decay)
            return tuple(acc[a] + w * d[a] for a in range(3))

        return lax.fori_loop(0, atoms // 8, step, start, unroll=atoms // 8)

    fields = [perm_part(l, OWN, (zero, zero, zero)) for l in range(beads)]
    for l in range(beads):
        for a in range(3):
            perm[l, a] = fields[l][a]

    for c in halo:
        c.wait_recv()
    for side in (LEFT, RIGHT):
        col[side] = pk[side].T

    for side in (OWN, LEFT, RIGHT):
        for a in range(3):
            spots = [pk[side, 4 * a + l : 4 * a + l + 1, :] for l in range(beads)]
            for dx in range(4):
                cps[dx, side, a : a + 1, :] = sum(fold[dx][l] * spots[l] for l in range(beads))
    sends = []
    for n, (turn, dx) in enumerate(others):
        sends.append(remote(cps.at[dx], cpin.at[n], cp_send.at[n], cp_recv.at[n], peer(turn, dx)))
        sends[-1].start()
    cp_copies = list(sends)

    for l in range(beads):
        acc = tuple(perm[l, a] for a in range(3))
        acc = perm_part(l, LEFT, acc)
        acc = perm_part(l, RIGHT, acc)
        for a in range(3):
            perm[l, a] = acc[a]
    rows = [
        jnp.concatenate([jnp.sum(perm[l, a], axis=0, keepdims=True) for a in range(3)], 0) for l in range(beads)
    ]
    for dx in range(4):
        fps[dx] = sum(fold[dx][l] * rows[l] for l in range(beads))
    fp_copies = []
    facing = {OWN: OWN, LEFT: RIGHT, RIGHT: LEFT}
    for turn, dx, side in around:
        n = (facing[side], turn * 4 + dx)
        fp_copies.append(remote(fps.at[dx], fpin.at[n], fp_send.at[n], fp_recv.at[n], peer(turn, dx, side)))
        fp_copies[-1].start()

    for c in cp_copies:
        c.wait_recv()
    for side in (OWN, LEFT, RIGHT):
        whole = cps[0, side]
        for n in range(len(others)):
            whole = whole + cpin[n, side]
        ctr[side, 0:3, :] = whole
        ctr[side, 3:8, :] = jnp.zeros((5, atoms), jnp.float32)
        ccol[side] = ctr[side].T

    target = [spread(ctr[OWN, a : a + 1, :]) for a in range(3)]
    for side in (OWN, LEFT, RIGHT):

        def step(i, carry, side=side):
            at = pl.ds(i * 8, 8)
            source = col[side, at, :]
            where = ccol[side, at, :]
            d = [target[a] - where[:, a : a + 1] for a in range(3)]
            r2 = d[0] * d[0] + d[1] * d[1] + d[2] * d[2]
            if side == OWN:
                r2 = jnp.where(moli == source[:, 14:15], CUT2, r2)
            r2 = jnp.minimum(r2, CUT2)
            inv = lax.rsqrt(r2)
            c = (r2 * gi) * source[:, 13:14] * (r2 * inv)
            decay = jnp.exp(c)
            damp3 = 1.0 - decay
            damp5 = damp3 + c * decay
            u = (CUT2 - r2) * (inv * (1.0 / CUT2))
            v = u * u * inv
            w3 = v * damp3
            w5 = (3.0 * v) * (inv * inv) * damp5
            e = [w5 * d[a] for a in range(3)]
            tens[side, 0, at, :] = e[0] * d[0] - w3
            tens[side, 1, at, :] = e[1] * d[1] - w3
            tens[side, 2, at, :] = e[2] * d[2] - w3
            tens[side, 3, at, :] = e[0] * d[1]
            tens[side, 4, at, :] = e[0] * d[2]
            tens[side, 5, at, :] = e[1] * d[2]
            return carry

        lax.fori_loop(0, atoms // 8, step, 0, unroll=atoms // 8)

    for c in fp_copies:
        c.wait_recv()
    fpin[OWN, 0] = fps[0]
    fields = [sum(fpin[side, n] for n in range(8)) for side in (OWN, LEFT, RIGHT)]
    cfield = fields[OWN]

    def induce_part(step_no, side, acc):
        def step(i, acc):
            at = pl.ds(i * 8, 8)
            m = mucol[side, at, :]
            m = [m[:, a : a + 1] for a in range(3)]
            t = [tens[side, n, at, :] for n in range(6)]
            return (
                acc[0] + (t[0] * m[0] + t[3] * m[1] + t[4] * m[2]),
                acc[1] + (t[3] * m[0] + t[1] * m[1] + t[5] * m[2]),
                acc[2] + (t[4] * m[0] + t[5] * m[1] + t[2] * m[2]),
            )

        return lax.fori_loop(0, atoms // 8, step, acc, unroll=atoms // 8)

    mu_copies = []
    dip_copies = []

    def columns(moment, side):
        wide = jnp.concatenate([moment, jnp.zeros((5, atoms), jnp.float32)], 0)
        mucol[side] = wide.T

    def rows_of(acc):
        return jnp.concatenate([jnp.sum(acc[a], axis=0, keepdims=True) for a in range(3)], 0)

    def induce_first():
        acc = (zero, zero, zero)
        for side in (OWN, LEFT, RIGHT):
            columns(pk[side, 15:16, :] * fields[side], side)
            acc = induce_part(0, side, acc)
        return rows_of(acc)

    def induce(n, moment):
        mu[n, OWN] = moment
        copies = [
            remote(mu.at[n, OWN], mu.at[n, RIGHT], mu_send.at[n, 0], mu_recv.at[n, 0], mu_left),
            remote(mu.at[n, OWN], mu.at[n, LEFT], mu_send.at[n, 1], mu_recv.at[n, 1], mu_right),
        ]
        for c in copies:
            c.start()
        mu_copies.extend(copies)
        if n == ITERS:
            for dx in (2, 1, 3):
                c = remote(mu.at[n, OWN], muin.at[dx], dip_send.at[dx], dip_recv.at[dx], peer(0, dx))
                c.start()
                dip_copies.append(c)

        columns(moment, OWN)
        acc = induce_part(n, OWN, (zero, zero, zero))
        for c, side in zip(copies, (RIGHT, LEFT)):
            c.wait_recv()
            columns(mu[n, side], side)
            acc = induce_part(n, side, acc)
        return rows_of(acc)

    moment = alpha * (cfield + induce_first())
    for n in range(1, ITERS):
        moment = alpha * (cfield + induce(n, moment))
    ind[...] = induce(ITERS, moment)
    ind_copies = []
    for dx in (2, 1, 3):
        c = remote(ind, indin.at[dx], ind_send.at[dx], ind_recv.at[dx], peer(0, dx))
        c.start()
        ind_copies.append(c)

    def put_moment(k, value):
        for a in range(3):
            moment_ref[a, pl.ds(k, 1), :] = value[a : a + 1]

    put_moment(spot, moment)
    total = [rows[l] + (8.0 * fold[0][l]) * ind[...] for l in range(beads)]
    for c, dx in zip(dip_copies, (2, 1, 3)):
        c.wait_recv()
        put_moment(lax.rem(spot + 4 - dx, 4), muin[dx])
    for c, dx in zip(ind_copies, (2, 1, 3)):
        c.wait_recv()
        total = [total[l] + (8.0 * fold[4 - dx][l]) * indin[dx] for l in range(beads)]
    for l in range(beads):
        for a in range(3):
            total_ref[a, l : l + 1, :] = total[l][a : a + 1]
    for c in halo + cp_copies + fp_copies + mu_copies + dip_copies + ind_copies:
        c.wait_send()


def solution(mesh):
    spaces = mesh.shape["space"]

    def body(positions, charges, polar, molecule):
        beads, _, atoms = positions.shape
        f32 = jnp.float32
        vmem = pl.BlockSpec(memory_space=pltpu.VMEM)
        dma = pltpu.SemaphoreType.DMA
        rounds = ITERS + 1
        total, moment = pl.pallas_call(
            functools.partial(kernel, beads, atoms, spaces),
            out_shape=(
                jax.ShapeDtypeStruct((3, beads, atoms), f32),
                jax.ShapeDtypeStruct((3, CONTR, atoms), f32),
            ),
            in_specs=[pl.BlockSpec(memory_space=pltpu.HBM)] * 4,
            out_specs=(vmem, vmem),
            scratch_shapes=[
                pltpu.VMEM((3, beads, atoms), f32),
                pltpu.VMEM((atoms,), f32), pltpu.VMEM((atoms,), f32), pltpu.VMEM((atoms,), jnp.int32),
                dma((4,)),
                pltpu.VMEM((3, 16, atoms), f32),
                pltpu.VMEM((3, atoms, 16), f32),
                pltpu.VMEM((beads, 3, 8, atoms), f32),
                pltpu.VMEM((4, 3, 3, atoms), f32),
                pltpu.VMEM((7, 3, 3, atoms), f32),
                pltpu.VMEM((4, 3, atoms), f32),
                pltpu.VMEM((3, 8, 3, atoms), f32),
                pltpu.VMEM((3, 8, atoms), f32),
                pltpu.VMEM((3, atoms, 8), f32),
                pltpu.VMEM((3, 6, atoms, atoms), f32),
                pltpu.VMEM((rounds, 3, 3, atoms), f32),
                pltpu.VMEM((3, atoms, 8), f32),
                pltpu.VMEM((3, atoms), f32),
                pltpu.VMEM((4, 3, atoms), f32),
                pltpu.VMEM((4, 3, atoms), f32),
                dma((2,)), dma((2,)),
                dma((7,)), dma((7,)),
                dma((3, 8)), dma((3, 8)),
                dma((rounds, 2)), dma((rounds, 2)),
                dma((4,)), dma((4,)),
                dma((4,)), dma((4,)),
            ],
            compiler_params=pltpu.CompilerParams(
                collective_id=0, has_side_effects=True, vmem_limit_bytes=60 * 1024 * 1024
            ),
            name="polarize",
        )(
            positions.transpose(1, 0, 2), charges, polar, molecule
        )
        return total.transpose(1, 0, 2), moment.transpose(1, 0, 2)

    in_specs = (P("bead", None, "space"), P("space"), P("space"), P("space"))
    out_specs = (P("bead", None, "space"), P(None, None, "space"))
    return jax.shard_map(body, mesh=mesh, in_specs=in_specs, out_specs=out_specs, check_vma=False)
```

```python
import functools
import math

import jax
import jax.numpy as jnp
import numpy as np
from jax import lax
from jax.experimental import pallas as pl
from jax.experimental.pallas import tpu as pltpu
from jax.sharding import PartitionSpec as P

BEADS = 32
CONTR = 4
ITERS = 2
CUT2 = 81.0
MESH = pl.DeviceIdType.MESH
OWN, NEAR, FAR = 0, 1, 2


def series(i):
    theta = 2.0 * math.pi * i / BEADS
    return (1.0 + 2.0 * math.cos(theta) + math.cos(2.0 * theta)) / BEADS


def kernel(
    beads, atoms, spaces,
    pos_hbm, charge_hbm, polar_hbm, mol_hbm,
    total_ref, moment_ref,
    pos_ref, charge_ref, polar_ref, mol_ref, in_sem, ready,
    pk, col, perm, cps, cpin, fps, fpin, ctr, ccol, tens, mu, mucol, ind, indin, muin,
    halo_send, halo_recv, cp_send, cp_recv, fp_send, fp_recv, mu_send, mu_recv,
    dip_send, dip_recv, ind_send, ind_recv,
):
    rank = lax.axis_index("bead")
    slab = lax.axis_index("space")
    half, spot = rank // 4, lax.rem(rank, 4)
    way = 1 - 2 * lax.rem(slab, 2)
    near, far = slab + way, lax.rem(slab - way + spaces, spaces)
    row_end = (lax.rem(slab, 8) == 0) | (lax.rem(slab, 8) == 7)
    across = (1 - half) * 4 + spot
    to_near = (rank, near)
    to_far = (rank, far)
    mu_far = (jnp.where(row_end, across, rank), far)
    slabs = (slab, near, far)

    def peer(turn, dx, side=OWN):
        return ((half if turn == 0 else 1 - half) * 4 + lax.rem(spot + dx, 4), slabs[side])

    others = [(turn, dx) for turn in (1, 0) for dx in (2, 1, 3, 0) if (turn, dx) != (0, 0)]
    around = [(turn, dx, side) for turn in (1, 0) for dx in (2, 1, 3, 0) for side in (FAR, NEAR, OWN)]
    around.remove((0, 0, OWN))
    barrier = pltpu.get_barrier_semaphore()
    greeted = [peer(1, 0), peer(1, 0, NEAR), peer(1, 0, FAR), to_near, to_far]
    row = [peer(0, dx) for dx in (2, 1, 3)]
    greeted += row
    for device in greeted:
        pl.semaphore_signal(barrier, inc=1, device_id=device, device_id_type=MESH)

    loads = [
        pltpu.make_async_copy(src, dst, in_sem.at[n])
        for n, (src, dst) in enumerate(
            ((pos_hbm, pos_ref), (charge_hbm, charge_ref), (polar_hbm, polar_ref), (mol_hbm, mol_ref))
        )
    ]
    for c in loads:
        c.start()

    def remote(src, dst, send, recv, device):
        return pltpu.make_async_remote_copy(
            src_ref=src, dst_ref=dst, send_sem=send, recv_sem=recv, device_id=device, device_id_type=MESH
        )

    def weight(k, l):
        j = lax.rem(2 * k - rank + 8, 8)
        value = jnp.float32(series(-l))
        for n in range(1, 8):
            value = jnp.where(j == n, jnp.float32(series(4 * n - l)), value)
        return value

    fold = [[weight(lax.rem(spot + dx, 4), l) for l in range(beads)] for dx in range(4)]
    for c in loads:
        c.wait()
    for a in range(3):
        pk[OWN, 4 * a : 4 * a + 4, :] = pos_ref[a]
    alpha = polar_ref[...].reshape(1, atoms)
    root = lax.rsqrt(alpha) * math.sqrt(0.39)
    pk[OWN, 12:13, :] = charge_ref[...].reshape(1, atoms) * (1.0 / (CUT2 * CUT2))
    pk[OWN, 13:14, :] = -root
    pk[OWN, 14:15, :] = mol_ref[...].astype(jnp.float32).reshape(1, atoms)
    pk[OWN, 15:16, :] = alpha

    pl.semaphore_wait(barrier, len(greeted))
    halo = [
        remote(pk.at[OWN], pk.at[NEAR], halo_send.at[0], halo_recv.at[0], to_near),
        remote(pk.at[OWN], pk.at[FAR], halo_send.at[1], halo_recv.at[1], to_far),
    ]
    for c in halo[::-1]:
        c.start()
    for device in row:
        pl.semaphore_signal(ready, inc=1, device_id=device, device_id_type=MESH)

    def spread(row):
        return jnp.broadcast_to(row, (8, atoms))

    col[OWN] = pk[OWN].T
    gi = spread(root)
    moli = spread(pk[OWN, 14:15, :])
    zero = jnp.zeros((8, atoms), jnp.float32)

    def perm_part(l, side, start):
        target = [spread(pk[OWN, 4 * a + l : 4 * a + l + 1, :]) for a in range(3)]

        def step(i, acc):
            source = col[side, pl.ds(i * 8, 8), :]
            d = [target[a] - source[:, 4 * a + l : 4 * a + l + 1] for a in range(3)]
            r2 = d[0] * d[0] + d[1] * d[1] + d[2] * d[2]
            if side == OWN:
                r2 = jnp.where(moli == source[:, 14:15], CUT2, r2)
            r2 = jnp.minimum(r2, CUT2)
            inv = lax.rsqrt(r2)
            c = (r2 * gi) * source[:, 13:14] * (r2 * inv)
            decay = jnp.exp(c)
            u = (CUT2 - r2) * inv
            w = (u * u) * (inv * source[:, 12:13]) * (1.0 - decay)
            return tuple(acc[a] + w * d[a] for a in range(3))

        return lax.fori_loop(0, atoms // 8, step, start, unroll=atoms // 8)

    fields = [perm_part(l, OWN, (zero, zero, zero)) for l in range(beads)]
    for l in range(beads):
        for a in range(3):
            perm[l, a] = fields[l][a]

    def perm_from(side):
        if side == NEAR:
            halo[0].wait_recv()
        col[side] = pk[side].T
        for l in range(beads):
            acc = perm_part(l, side, tuple(perm[l, a] for a in range(3)))
            for a in range(3):
                perm[l, a] = acc[a]

    perm_from(NEAR)
    halo[1].wait_recv()
    for side in (OWN, NEAR, FAR):
        for a in range(3):
            spots = [pk[side, 4 * a + l : 4 * a + l + 1, :] for l in range(beads)]
            for dx in range(4):
                cps[dx, side, a : a + 1, :] = sum(fold[dx][l] * spots[l] for l in range(beads))
    pl.semaphore_wait(ready, len(row))
    sends = []
    for n, (turn, dx) in enumerate(others):
        sends.append(remote(cps.at[dx], cpin.at[n], cp_send.at[n], cp_recv.at[n], peer(turn, dx)))
        sends[-1].start()
    cp_copies = list(sends)

    perm_from(FAR)
    rows = [
        jnp.concatenate([jnp.sum(perm[l, a], axis=0, keepdims=True) for a in range(3)], 0) for l in range(beads)
    ]
    for dx in range(4):
        fps[dx] = sum(fold[dx][l] * rows[l] for l in range(beads))
    fp_copies = []
    for turn, dx, side in around:
        n = (side, turn * 4 + dx)
        fp_copies.append(remote(fps.at[dx], fpin.at[n], fp_send.at[n], fp_recv.at[n], peer(turn, dx, side)))
        fp_copies[-1].start()

    for c in cp_copies:
        c.wait_recv()
    for side in (OWN, NEAR, FAR):
        whole = cps[0, side]
        for n in range(len(others)):
            whole = whole + cpin[n, side]
        ctr[side, 0:3, :] = whole
        ctr[side, 3:8, :] = jnp.zeros((5, atoms), jnp.float32)
        ccol[side] = ctr[side].T

    target = [spread(ctr[OWN, a : a + 1, :]) for a in range(3)]
    for side in (OWN, NEAR, FAR):

        def step(i, carry, side=side):
            at = pl.ds(i * 8, 8)
            source = col[side, at, :]
            where = ccol[side, at, :]
            d = [target[a] - where[:, a : a + 1] for a in range(3)]
            r2 = d[0] * d[0] + d[1] * d[1] + d[2] * d[2]
            if side == OWN:
                r2 = jnp.where(moli == source[:, 14:15], CUT2, r2)
            r2 = jnp.minimum(r2, CUT2)
            inv = lax.rsqrt(r2)
            c = (r2 * gi) * source[:, 13:14] * (r2 * inv)
            decay = jnp.exp(c)
            damp3 = 1.0 - decay
            damp5 = damp3 + c * decay
            u = (CUT2 - r2) * inv
            lift = jnp.maximum(inv * damp5, 1e-30)
            stretch = (u * inv) * (lift * lax.rsqrt(lift))
            for a in range(3):
                tens[side, a, at, :] = stretch * d[a]
            tens[side, 3, at, :] = (u * u) * inv * (damp3 * (1.0 / 3.0))
            return carry

        lax.fori_loop(0, atoms // 8, step, 0, unroll=atoms // 8)

    for c in fp_copies:
        c.wait_recv()
    fpin[OWN, 0] = fps[0]
    fields = [sum(fpin[side, n] for n in range(8)) for side in (OWN, NEAR, FAR)]
    cfield = fields[OWN]

    def induce_part(step_no, side, acc):
        def step(i, acc):
            at = pl.ds(i * 8, 8)
            m = mucol[side, at, :]
            m = [m[:, a : a + 1] for a in range(3)]
            f = [tens[side, a, at, :] for a in range(3)]
            flat = tens[side, 3, at, :]
            along = f[0] * m[0] + f[1] * m[1] + f[2] * m[2]
            return tuple(acc[a] + (f[a] * along - flat * m[a]) for a in range(3))

        return lax.fori_loop(0, atoms // 8, step, acc, unroll=atoms // 8)

    mu_copies = []
    dip_copies = []

    def columns(moment, side):
        wide = jnp.concatenate([moment, jnp.zeros((5, atoms), jnp.float32)], 0)
        mucol[side] = wide.T

    def rows_of(acc):
        total = jnp.concatenate([jnp.sum(acc[a], axis=0, keepdims=True) for a in range(3)], 0)
        return total * (3.0 / (CUT2 * CUT2))

    def induce_first():
        acc = (zero, zero, zero)
        for side in (OWN, NEAR, FAR):
            columns(pk[side, 15:16, :] * fields[side], side)
            acc = induce_part(0, side, acc)
        return rows_of(acc)

    def induce(n, moment):
        mu[n, OWN] = moment
        copies = [
            remote(mu.at[n, OWN], mu.at[n, NEAR], mu_send.at[n, 0], mu_recv.at[n, 0], to_near),
            remote(mu.at[n, OWN], mu.at[n, FAR], mu_send.at[n, 1], mu_recv.at[n, 1], mu_far),
        ]
        for c in copies[::-1]:
            c.start()
        mu_copies.extend(copies)
        if n == ITERS:
            for dx in (2, 1, 3):
                c = remote(mu.at[n, OWN], muin.at[dx], dip_send.at[dx], dip_recv.at[dx], peer(0, dx))
                c.start()
                dip_copies.append(c)

        columns(moment, OWN)
        acc = induce_part(n, OWN, (zero, zero, zero))
        for c, side in zip(copies, (NEAR, FAR)):
            c.wait_recv()
            columns(mu[n, side], side)
            acc = induce_part(n, side, acc)
        return rows_of(acc)

    moment = alpha * (cfield + induce_first())
    for n in range(1, ITERS):
        moment = alpha * (cfield + induce(n, moment))
    ind[...] = induce(ITERS, moment)
    ind_copies = []
    for dx in (2, 1, 3):
        c = remote(ind, indin.at[dx], ind_send.at[dx], ind_recv.at[dx], peer(0, dx))
        c.start()
        ind_copies.append(c)

    def put_moment(k, value):
        for a in range(3):
            moment_ref[a, pl.ds(k, 1), :] = value[a : a + 1]

    put_moment(spot, moment)
    total = [rows[l] + (8.0 * fold[0][l]) * ind[...] for l in range(beads)]
    for c, dx in zip(dip_copies, (2, 1, 3)):
        c.wait_recv()
        put_moment(lax.rem(spot + 4 - dx, 4), muin[dx])
    for c, dx in zip(ind_copies, (2, 1, 3)):
        c.wait_recv()
        total = [total[l] + (8.0 * fold[4 - dx][l]) * indin[dx] for l in range(beads)]
    for l in range(beads):
        for a in range(3):
            total_ref[a, l : l + 1, :] = total[l][a : a + 1]
    for c in halo + cp_copies + fp_copies + mu_copies + dip_copies + ind_copies:
        c.wait_send()


def solution(mesh):
    spaces = mesh.shape["space"]

    def body(positions, charges, polar, molecule):
        beads, _, atoms = positions.shape
        f32 = jnp.float32
        vmem = pl.BlockSpec(memory_space=pltpu.VMEM)
        dma = pltpu.SemaphoreType.DMA
        rounds = ITERS + 1
        total, moment = pl.pallas_call(
            functools.partial(kernel, beads, atoms, spaces),
            out_shape=(
                jax.ShapeDtypeStruct((3, beads, atoms), f32),
                jax.ShapeDtypeStruct((3, CONTR, atoms), f32),
            ),
            in_specs=[pl.BlockSpec(memory_space=pltpu.HBM)] * 4,
            out_specs=(vmem, vmem),
            scratch_shapes=[
                pltpu.VMEM((3, beads, atoms), f32),
                pltpu.VMEM((atoms,), f32), pltpu.VMEM((atoms,), f32), pltpu.VMEM((atoms,), jnp.int32),
                dma((4,)),
                pltpu.SemaphoreType.REGULAR,
                pltpu.VMEM((3, 16, atoms), f32),
                pltpu.VMEM((3, atoms, 16), f32),
                pltpu.VMEM((beads, 3, 8, atoms), f32),
                pltpu.VMEM((4, 3, 3, atoms), f32),
                pltpu.VMEM((7, 3, 3, atoms), f32),
                pltpu.VMEM((4, 3, atoms), f32),
                pltpu.VMEM((3, 8, 3, atoms), f32),
                pltpu.VMEM((3, 8, atoms), f32),
                pltpu.VMEM((3, atoms, 8), f32),
                pltpu.VMEM((3, 4, atoms, atoms), f32),
                pltpu.VMEM((rounds, 3, 3, atoms), f32),
                pltpu.VMEM((3, atoms, 8), f32),
                pltpu.VMEM((3, atoms), f32),
                pltpu.VMEM((4, 3, atoms), f32),
                pltpu.VMEM((4, 3, atoms), f32),
                dma((2,)), dma((2,)),
                dma((7,)), dma((7,)),
                dma((3, 8)), dma((3, 8)),
                dma((rounds, 2)), dma((rounds, 2)),
                dma((4,)), dma((4,)),
                dma((4,)), dma((4,)),
            ],
            compiler_params=pltpu.CompilerParams(
                collective_id=0, has_side_effects=True, vmem_limit_bytes=60 * 1024 * 1024
            ),
            name="polarize",
        )(
            positions.transpose(1, 0, 2), charges, polar, molecule
        )
        return total.transpose(1, 0, 2), moment.transpose(1, 0, 2)

    in_specs = (P("bead", None, "space"), P("space"), P("space"), P("space"))
    out_specs = (P("bead", None, "space"), P(None, None, "space"))
    return jax.shard_map(body, mesh=mesh, in_specs=in_specs, out_specs=out_specs, check_vma=False)
```

```python
import functools
import math

import jax
import jax.numpy as jnp
import numpy as np
from jax import lax
from jax.experimental import pallas as pl
from jax.experimental.pallas import tpu as pltpu
from jax.sharding import PartitionSpec as P

BEADS = 32
CONTR = 4
ITERS = 2
CUT2 = 81.0
MESH = pl.DeviceIdType.MESH
OWN, NEAR, FAR = 0, 1, 2


def series(i):
    theta = 2.0 * math.pi * i / BEADS
    return (1.0 + 2.0 * math.cos(theta) + math.cos(2.0 * theta)) / BEADS


def kernel(
    beads, atoms, spaces,
    pos_hbm, charge_hbm, polar_hbm, mol_hbm,
    total_ref, moment_ref,
    pos_ref, charge_ref, polar_ref, mol_ref, in_sem, ready,
    pk, col, perm, cps, cpin, fps, fpin, ctr, ccol, tens, mu, mucol, ind, indin, muin,
    halo_send, halo_recv, cp_send, cp_recv, fp_send, fp_recv, mu_send, mu_recv,
    dip_send, dip_recv, ind_send, ind_recv,
):
    rank = lax.axis_index("bead")
    slab = lax.axis_index("space")
    half, spot = rank // 4, lax.rem(rank, 4)
    way = 1 - 2 * lax.rem(slab, 2)
    near, far = slab + way, lax.rem(slab - way + spaces, spaces)
    row_end = (lax.rem(slab, 8) == 0) | (lax.rem(slab, 8) == 7)
    across = (1 - half) * 4 + spot
    to_near = (rank, near)
    to_far = (rank, far)
    mu_far = (jnp.where(row_end, across, rank), far)
    slabs = (slab, near, far)

    def peer(turn, dx, side=OWN):
        return ((half if turn == 0 else 1 - half) * 4 + lax.rem(spot + dx, 4), slabs[side])

    others = [(turn, dx) for turn in (1, 0) for dx in (2, 1, 3, 0) if (turn, dx) != (0, 0)]
    around = [(turn, dx, side) for turn in (1, 0) for dx in (2, 1, 3, 0) for side in (FAR, NEAR, OWN)]
    around.remove((0, 0, OWN))
    barrier = pltpu.get_barrier_semaphore()
    greeted = [peer(1, 0), peer(1, 0, NEAR), peer(1, 0, FAR), to_near, to_far]
    row = [peer(0, dx) for dx in (2, 1, 3)]
    greeted += row
    for device in greeted:
        pl.semaphore_signal(barrier, inc=1, device_id=device, device_id_type=MESH)

    loads = [
        pltpu.make_async_copy(src, dst, in_sem.at[n])
        for n, (src, dst) in enumerate(
            ((pos_hbm, pos_ref), (charge_hbm, charge_ref), (polar_hbm, polar_ref), (mol_hbm, mol_ref))
        )
    ]
    for c in loads:
        c.start()

    def remote(src, dst, send, recv, device):
        return pltpu.make_async_remote_copy(
            src_ref=src, dst_ref=dst, send_sem=send, recv_sem=recv, device_id=device, device_id_type=MESH
        )

    def weight(k, l):
        j = lax.rem(2 * k - rank + 8, 8)
        value = jnp.float32(series(-l))
        for n in range(1, 8):
            value = jnp.where(j == n, jnp.float32(series(4 * n - l)), value)
        return value

    fold = [[weight(lax.rem(spot + dx, 4), l) for l in range(beads)] for dx in range(4)]
    for c in loads:
        c.wait()
    for a in range(3):
        pk[OWN, 4 * a : 4 * a + 4, :] = pos_ref[a]
    alpha = polar_ref[...].reshape(1, atoms)
    root = lax.rsqrt(alpha) * math.sqrt(0.39)
    pk[OWN, 12:13, :] = charge_ref[...].reshape(1, atoms) * (1.0 / (CUT2 * CUT2))
    pk[OWN, 13:14, :] = -root
    pk[OWN, 14:15, :] = mol_ref[...].astype(jnp.float32).reshape(1, atoms)
    pk[OWN, 15:16, :] = alpha

    pl.semaphore_wait(barrier, len(greeted))
    halo = [
        remote(pk.at[OWN], pk.at[NEAR], halo_send.at[0], halo_recv.at[0], to_near),
        remote(pk.at[OWN], pk.at[FAR], halo_send.at[1], halo_recv.at[1], to_far),
    ]
    for c in halo[::-1]:
        c.start()
    for device in row:
        pl.semaphore_signal(ready, inc=1, device_id=device, device_id_type=MESH)

    def spread(row):
        return jnp.broadcast_to(row, (8, atoms))

    col[OWN] = pk[OWN].T
    gi = spread(root)
    moli = spread(pk[OWN, 14:15, :])
    zero = jnp.zeros((8, atoms), jnp.float32)

    def perm_part(l, side, start):
        target = [spread(pk[OWN, 4 * a + l : 4 * a + l + 1, :]) for a in range(3)]

        def step(i, acc):
            source = col[side, pl.ds(i * 8, 8), :]
            d = [target[a] - source[:, 4 * a + l : 4 * a + l + 1] for a in range(3)]
            r2 = d[0] * d[0] + d[1] * d[1] + d[2] * d[2]
            if side == OWN:
                r2 = jnp.where(moli == source[:, 14:15], CUT2, r2)
            r2 = jnp.minimum(r2, CUT2)
            inv = lax.rsqrt(r2)
            c = (r2 * gi) * source[:, 13:14] * (r2 * inv)
            decay = jnp.exp(c)
            u = (CUT2 - r2) * inv
            w = (u * u) * (inv * source[:, 12:13]) * (1.0 - decay)
            return tuple(acc[a] + w * d[a] for a in range(3))

        return lax.fori_loop(0, atoms // 8, step, start, unroll=atoms // 8)

    fields = [perm_part(l, OWN, (zero, zero, zero)) for l in range(beads)]
    for l in range(beads):
        for a in range(3):
            perm[l, a] = fields[l][a]

    def perm_from(side):
        if side == NEAR:
            halo[0].wait_recv()
        col[side] = pk[side].T
        for l in range(beads):
            acc = perm_part(l, side, tuple(perm[l, a] for a in range(3)))
            for a in range(3):
                perm[l, a] = acc[a]

    perm_from(NEAR)
    halo[1].wait_recv()
    for side in (OWN, NEAR, FAR):
        for a in range(3):
            spots = [pk[side, 4 * a + l : 4 * a + l + 1, :] for l in range(beads)]
            for dx in range(4):
                cps[dx, side, a : a + 1, :] = sum(fold[dx][l] * spots[l] for l in range(beads))
    pl.semaphore_wait(ready, len(row))
    sends = []
    for n, (turn, dx) in enumerate(others):
        sends.append(remote(cps.at[dx], cpin.at[n], cp_send.at[n], cp_recv.at[n], peer(turn, dx)))
        sends[-1].start()
    cp_copies = list(sends)

    perm_from(FAR)
    rows = [
        jnp.concatenate([jnp.sum(perm[l, a], axis=0, keepdims=True) for a in range(3)], 0) for l in range(beads)
    ]
    for dx in range(4):
        fps[dx] = sum(fold[dx][l] * rows[l] for l in range(beads))
    fp_copies = []
    for turn, dx, side in around:
        n = (side, turn * 4 + dx)
        fp_copies.append(remote(fps.at[dx], fpin.at[n], fp_send.at[n], fp_recv.at[n], peer(turn, dx, side)))
        fp_copies[-1].start()

    for c in cp_copies:
        c.wait_recv()
    for side in (OWN, NEAR, FAR):
        whole = cps[0, side]
        for n in range(len(others)):
            whole = whole + cpin[n, side]
        ctr[side, 0:3, :] = whole
        ctr[side, 3:8, :] = jnp.zeros((5, atoms), jnp.float32)
        ccol[side] = ctr[side].T

    target = [spread(ctr[OWN, a : a + 1, :]) for a in range(3)]
    for side in (OWN, NEAR, FAR):

        def step(i, carry, side=side):
            at = pl.ds(i * 8, 8)
            source = col[side, at, :]
            where = ccol[side, at, :]
            d = [target[a] - where[:, a : a + 1] for a in range(3)]
            r2 = d[0] * d[0] + d[1] * d[1] + d[2] * d[2]
            if side == OWN:
                r2 = jnp.where(moli == source[:, 14:15], CUT2, r2)
            r2 = jnp.minimum(r2, CUT2)
            inv = lax.rsqrt(r2)
            c = (r2 * gi) * source[:, 13:14] * (r2 * inv)
            decay = jnp.exp(c)
            damp3 = 1.0 - decay
            damp5 = damp3 + c * decay
            u = (CUT2 - r2) * inv
            lift = jnp.maximum(inv * damp5, 1e-30)
            stretch = (u * inv) * (lift * lax.rsqrt(lift))
            for a in range(3):
                tens[side, a, at, :] = stretch * d[a]
            tens[side, 3, at, :] = (u * u) * inv * (damp3 * (1.0 / 3.0))
            return carry

        lax.fori_loop(0, atoms // 8, step, 0, unroll=atoms // 8)

    for c in fp_copies:
        c.wait_recv()
    fpin[OWN, 0] = fps[0]
    fields = [sum(fpin[side, n] for n in range(8)) for side in (OWN, NEAR, FAR)]
    cfield = fields[OWN]

    def induce_part(step_no, side, acc):
        def step(i, acc):
            at = pl.ds(i * 8, 8)
            m = mucol[side, at, :]
            m = [m[:, a : a + 1] for a in range(3)]
            f = [tens[side, a, at, :] for a in range(3)]
            flat = tens[side, 3, at, :]
            along = f[0] * m[0] + f[1] * m[1] + f[2] * m[2]
            return tuple(acc[a] + (f[a] * along - flat * m[a]) for a in range(3))

        return lax.fori_loop(0, atoms // 8, step, acc, unroll=atoms // 8)

    mu_copies = []
    dip_copies = []

    def columns(moment, side):
        wide = jnp.concatenate([moment, jnp.zeros((5, atoms), jnp.float32)], 0)
        mucol[side] = wide.T

    def rows_of(acc):
        total = jnp.concatenate([jnp.sum(acc[a], axis=0, keepdims=True) for a in range(3)], 0)
        return total * (3.0 / (CUT2 * CUT2))

    def induce_first():
        acc = (zero, zero, zero)
        for side in (OWN, NEAR, FAR):
            columns(pk[side, 15:16, :] * fields[side], side)
            acc = induce_part(0, side, acc)
        return rows_of(acc)

    def induce(n, moment):
        mu[n, OWN] = moment
        copies = [
            remote(mu.at[n, OWN], mu.at[n, NEAR], mu_send.at[n, 0], mu_recv.at[n, 0], to_near),
            remote(mu.at[n, OWN], mu.at[n, FAR], mu_send.at[n, 1], mu_recv.at[n, 1], mu_far),
        ]
        for c in copies[::-1]:
            c.start()
        mu_copies.extend(copies)
        if n == ITERS:
            for dx in (2, 1, 3):
                c = remote(mu.at[n, OWN], muin.at[dx], dip_send.at[dx], dip_recv.at[dx], peer(0, dx))
                c.start()
                dip_copies.append(c)

        columns(moment, OWN)
        acc = induce_part(n, OWN, (zero, zero, zero))
        for c, side in zip(copies, (NEAR, FAR)):
            c.wait_recv()
            columns(mu[n, side], side)
            acc = induce_part(n, side, acc)
        return rows_of(acc)

    moment = alpha * (cfield + induce_first())
    for n in range(1, ITERS):
        moment = alpha * (cfield + induce(n, moment))
    ind[...] = induce(ITERS, moment)
    ind_copies = []
    for dx in (2, 1, 3):
        c = remote(ind, indin.at[dx], ind_send.at[dx], ind_recv.at[dx], peer(0, dx))
        c.start()
        ind_copies.append(c)

    def put_moment(k, value):
        for a in range(3):
            moment_ref[a, pl.ds(k, 1), :] = value[a : a + 1]

    put_moment(spot, moment)
    total = [rows[l] + (8.0 * fold[0][l]) * ind[...] for l in range(beads)]
    for c, dx in zip(dip_copies, (2, 1, 3)):
        c.wait_recv()
        put_moment(lax.rem(spot + 4 - dx, 4), muin[dx])
    for c, dx in zip(ind_copies, (2, 1, 3)):
        c.wait_recv()
        total = [total[l] + (8.0 * fold[4 - dx][l]) * indin[dx] for l in range(beads)]
    for l in range(beads):
        for a in range(3):
            total_ref[a, l : l + 1, :] = total[l][a : a + 1]
    for c in halo + cp_copies + fp_copies + mu_copies + dip_copies + ind_copies:
        c.wait_send()


def solution(mesh):
    spaces = mesh.shape["space"]

    def body(positions, charges, polar, molecule):
        beads, _, atoms = positions.shape
        f32 = jnp.float32
        vmem = pl.BlockSpec(memory_space=pltpu.VMEM)
        dma = pltpu.SemaphoreType.DMA
        rounds = ITERS + 1
        total, moment = pl.pallas_call(
            functools.partial(kernel, beads, atoms, spaces),
            out_shape=(
                jax.ShapeDtypeStruct((3, beads, atoms), f32),
                jax.ShapeDtypeStruct((3, CONTR, atoms), f32),
            ),
            in_specs=[pl.BlockSpec(memory_space=pltpu.HBM)] * 4,
            out_specs=(vmem, vmem),
            scratch_shapes=[
                pltpu.VMEM((3, beads, atoms), f32),
                pltpu.VMEM((atoms,), f32), pltpu.VMEM((atoms,), f32), pltpu.VMEM((atoms,), jnp.int32),
                dma((4,)),
                pltpu.SemaphoreType.REGULAR,
                pltpu.VMEM((3, 16, atoms), f32),
                pltpu.VMEM((3, atoms, 16), f32),
                pltpu.VMEM((beads, 3, 8, atoms), f32),
                pltpu.VMEM((4, 3, 3, atoms), f32),
                pltpu.VMEM((7, 3, 3, atoms), f32),
                pltpu.VMEM((4, 3, atoms), f32),
                pltpu.VMEM((3, 8, 3, atoms), f32),
                pltpu.VMEM((3, 8, atoms), f32),
                pltpu.VMEM((3, atoms, 8), f32),
                pltpu.VMEM((3, 4, atoms, atoms), f32),
                pltpu.VMEM((rounds, 3, 3, atoms), f32),
                pltpu.VMEM((3, atoms, 8), f32),
                pltpu.VMEM((3, atoms), f32),
                pltpu.VMEM((4, 3, atoms), f32),
                pltpu.VMEM((4, 3, atoms), f32),
                dma((2,)), dma((2,)),
                dma((7,)), dma((7,)),
                dma((3, 8)), dma((3, 8)),
                dma((rounds, 2)), dma((rounds, 2)),
                dma((4,)), dma((4,)),
                dma((4,)), dma((4,)),
            ],
            compiler_params=pltpu.CompilerParams(
                collective_id=0, has_side_effects=True, vmem_limit_bytes=40 * 1024 * 1024
            ),
            name="polarize",
        )(
            *[
                pltpu.with_memory_space_constraint(x, pltpu.HBM)
                for x in (positions.transpose(1, 0, 2), charges, polar, molecule)
            ]
        )
        return total.transpose(1, 0, 2), moment.transpose(1, 0, 2)

    in_specs = (P("bead", None, "space"), P("space"), P("space"), P("space"))
    out_specs = (P("bead", None, "space"), P(None, None, "space"))
    return jax.shard_map(body, mesh=mesh, in_specs=in_specs, out_specs=out_specs, check_vma=False)
```

```python
import functools
import math

import jax
import jax.numpy as jnp
import numpy as np
from jax import lax
from jax.experimental import pallas as pl
from jax.experimental.pallas import tpu as pltpu
from jax.sharding import PartitionSpec as P

BEADS = 32
CONTR = 4
ITERS = 2
CUT2 = 81.0
MESH = pl.DeviceIdType.MESH
OWN, NEAR, FAR = 0, 1, 2


def series(i):
    theta = 2.0 * math.pi * i / BEADS
    return (1.0 + 2.0 * math.cos(theta) + math.cos(2.0 * theta)) / BEADS


def kernel(
    beads, atoms, spaces,
    pos_hbm, charge_hbm, polar_hbm, mol_hbm,
    total_ref, moment_ref,
    pos_ref, charge_ref, polar_ref, mol_ref, in_sem, ready,
    pk, col, perm, cps, cpin, fps, fpin, ctr, ccol, tens, mu, mucol, ind, indin, muin,
    halo_send, halo_recv, cp_send, cp_recv, fp_send, fp_recv, mu_send, mu_recv,
    dip_send, dip_recv, ind_send, ind_recv,
):
    rank = lax.axis_index("bead")
    slab = lax.axis_index("space")
    half, spot = rank // 4, lax.rem(rank, 4)
    way = 1 - 2 * lax.rem(slab, 2)
    near, far = slab + way, lax.rem(slab - way + spaces, spaces)
    row_end = (lax.rem(slab, 8) == 0) | (lax.rem(slab, 8) == 7)
    across = (1 - half) * 4 + spot
    to_near = (rank, near)
    to_far = (rank, far)
    mu_far = (jnp.where(row_end, across, rank), far)
    slabs = (slab, near, far)

    def peer(turn, dx, side=OWN):
        return ((half if turn == 0 else 1 - half) * 4 + lax.rem(spot + dx, 4), slabs[side])

    others = [(turn, dx) for turn in (1, 0) for dx in (2, 1, 3, 0) if (turn, dx) != (0, 0)]
    around = [(turn, dx, side) for side in (OWN, NEAR, FAR) for turn in (1, 0) for dx in (2, 1, 3, 0)]
    around.remove((0, 0, OWN))
    barrier = pltpu.get_barrier_semaphore()
    greeted = [peer(1, 0), peer(1, 0, NEAR), peer(1, 0, FAR), to_near, to_far]
    row = [peer(0, dx) for dx in (2, 1, 3)]
    greeted += row
    for device in greeted:
        pl.semaphore_signal(barrier, inc=1, device_id=device, device_id_type=MESH)

    loads = [
        pltpu.make_async_copy(src, dst, in_sem.at[n])
        for n, (src, dst) in enumerate(
            ((pos_hbm, pos_ref), (charge_hbm, charge_ref), (polar_hbm, polar_ref), (mol_hbm, mol_ref))
        )
    ]
    for c in loads:
        c.start()

    def remote(src, dst, send, recv, device):
        return pltpu.make_async_remote_copy(
            src_ref=src, dst_ref=dst, send_sem=send, recv_sem=recv, device_id=device, device_id_type=MESH
        )

    def weight(k, l):
        j = lax.rem(2 * k - rank + 8, 8)
        value = jnp.float32(series(-l))
        for n in range(1, 8):
            value = jnp.where(j == n, jnp.float32(series(4 * n - l)), value)
        return value

    fold = [[weight(lax.rem(spot + dx, 4), l) for l in range(beads)] for dx in range(4)]
    for c in loads:
        c.wait()
    for a in range(3):
        pk[OWN, 4 * a : 4 * a + 4, :] = pos_ref[a]
    alpha = polar_ref[...].reshape(1, atoms)
    root = lax.rsqrt(alpha) * math.sqrt(0.39)
    pk[OWN, 12:13, :] = charge_ref[...].reshape(1, atoms) * (1.0 / (CUT2 * CUT2))
    pk[OWN, 13:14, :] = -root
    pk[OWN, 14:15, :] = mol_ref[...].astype(jnp.float32).reshape(1, atoms)
    pk[OWN, 15:16, :] = alpha

    pl.semaphore_wait(barrier, len(greeted))
    halo = [
        remote(pk.at[OWN], pk.at[NEAR], halo_send.at[0], halo_recv.at[0], to_near),
        remote(pk.at[OWN], pk.at[FAR], halo_send.at[1], halo_recv.at[1], to_far),
    ]
    for c in halo[::-1]:
        c.start()
    for device in row:
        pl.semaphore_signal(ready, inc=1, device_id=device, device_id_type=MESH)

    def spread(row):
        return jnp.broadcast_to(row, (8, atoms))

    col[OWN] = pk[OWN].T
    gi = spread(root)
    moli = spread(pk[OWN, 14:15, :])
    zero = jnp.zeros((8, atoms), jnp.float32)

    def perm_part(l, side, start):
        target = [spread(pk[OWN, 4 * a + l : 4 * a + l + 1, :]) for a in range(3)]

        def step(i, acc):
            source = col[side, pl.ds(i * 8, 8), :]
            d = [target[a] - source[:, 4 * a + l : 4 * a + l + 1] for a in range(3)]
            r2 = d[0] * d[0] + d[1] * d[1] + d[2] * d[2]
            if side == OWN:
                r2 = jnp.where(moli == source[:, 14:15], CUT2, r2)
            r2 = jnp.minimum(r2, CUT2)
            inv = lax.rsqrt(r2)
            c = (r2 * gi) * source[:, 13:14] * (r2 * inv)
            decay = jnp.exp(c)
            u = (CUT2 - r2) * inv
            w = (u * u) * (inv * source[:, 12:13]) * (1.0 - decay)
            return tuple(acc[a] + w * d[a] for a in range(3))

        return lax.fori_loop(0, atoms // 8, step, start, unroll=atoms // 8)

    fields = [perm_part(l, OWN, (zero, zero, zero)) for l in range(beads)]
    for l in range(beads):
        for a in range(3):
            perm[l, a] = fields[l][a]

    def perm_from(side):
        if side == NEAR:
            halo[0].wait_recv()
        col[side] = pk[side].T
        for l in range(beads):
            acc = perm_part(l, side, tuple(perm[l, a] for a in range(3)))
            for a in range(3):
                perm[l, a] = acc[a]

    def contract_spots(side):
        for a in range(3):
            spots = [pk[side, 4 * a + l : 4 * a + l + 1, :] for l in range(beads)]
            for dx in range(4):
                cps[dx, side, a : a + 1, :] = sum(fold[dx][l] * spots[l] for l in range(beads))

    perm_from(NEAR)
    contract_spots(OWN)
    contract_spots(NEAR)
    halo[1].wait_recv()
    contract_spots(FAR)
    pl.semaphore_wait(ready, len(row))
    sends = []
    for n, (turn, dx) in enumerate(others):
        sends.append(remote(cps.at[dx], cpin.at[n], cp_send.at[n], cp_recv.at[n], peer(turn, dx)))
        sends[-1].start()
    cp_copies = list(sends)

    perm_from(FAR)
    rows = [
        jnp.concatenate([jnp.sum(perm[l, a], axis=0, keepdims=True) for a in range(3)], 0) for l in range(beads)
    ]
    for dx in range(4):
        fps[dx] = sum(fold[dx][l] * rows[l] for l in range(beads))
    fp_copies = []
    for turn, dx, side in around:
        n = (side, turn * 4 + dx)
        fp_copies.append(remote(fps.at[dx], fpin.at[n], fp_send.at[n], fp_recv.at[n], peer(turn, dx, side)))
        fp_copies[-1].start()

    for c in cp_copies:
        c.wait_recv()
    for side in (OWN, NEAR, FAR):
        whole = cps[0, side]
        for n in range(len(others)):
            whole = whole + cpin[n, side]
        ctr[side, 0:3, :] = whole
        ctr[side, 3:8, :] = jnp.zeros((5, atoms), jnp.float32)
        ccol[side] = ctr[side].T

    target = [spread(ctr[OWN, a : a + 1, :]) for a in range(3)]
    for side in (OWN, NEAR, FAR):

        def step(i, carry, side=side):
            at = pl.ds(i * 8, 8)
            source = col[side, at, :]
            where = ccol[side, at, :]
            d = [target[a] - where[:, a : a + 1] for a in range(3)]
            r2 = d[0] * d[0] + d[1] * d[1] + d[2] * d[2]
            if side == OWN:
                r2 = jnp.where(moli == source[:, 14:15], CUT2, r2)
            r2 = jnp.minimum(r2, CUT2)
            inv = lax.rsqrt(r2)
            c = (r2 * gi) * source[:, 13:14] * (r2 * inv)
            decay = jnp.exp(c)
            damp3 = 1.0 - decay
            damp5 = damp3 + c * decay
            u = (CUT2 - r2) * inv
            lift = jnp.maximum(inv * damp5, 1e-30)
            stretch = (u * inv) * (lift * lax.rsqrt(lift))
            for a in range(3):
                tens[side, a, at, :] = stretch * d[a]
            tens[side, 3, at, :] = (u * u) * inv * (damp3 * (1.0 / 3.0))
            return carry

        lax.fori_loop(0, atoms // 8, step, 0, unroll=atoms // 8)

    def induce_part(step_no, side, acc):
        def step(i, acc):
            at = pl.ds(i * 8, 8)
            m = mucol[side, at, :]
            m = [m[:, a : a + 1] for a in range(3)]
            f = [tens[side, a, at, :] for a in range(3)]
            flat = tens[side, 3, at, :]
            along = f[0] * m[0] + f[1] * m[1] + f[2] * m[2]
            return tuple(acc[a] + (f[a] * along - flat * m[a]) for a in range(3))

        return lax.fori_loop(0, atoms // 8, step, acc, unroll=atoms // 8)

    mu_copies = []
    dip_copies = []

    def columns(moment, side):
        wide = jnp.concatenate([moment, jnp.zeros((5, atoms), jnp.float32)], 0)
        mucol[side] = wide.T

    def rows_of(acc):
        total = jnp.concatenate([jnp.sum(acc[a], axis=0, keepdims=True) for a in range(3)], 0)
        return total * (3.0 / (CUT2 * CUT2))

    def cfield_of(side):
        parts = [fps[0]] if side == OWN else []
        for c, (turn, dx, at) in zip(fp_copies, around):
            if at == side:
                c.wait_recv()
                parts.append(fpin[side, turn * 4 + dx])
        return sum(parts)

    cfield = cfield_of(OWN)
    columns(alpha * cfield, OWN)
    first = induce_part(0, OWN, (zero, zero, zero))
    for side in (NEAR, FAR):
        columns(pk[side, 15:16, :] * cfield_of(side), side)
        first = induce_part(0, side, first)

    def induce(n, moment):
        mu[n, OWN] = moment
        copies = [
            remote(mu.at[n, OWN], mu.at[n, NEAR], mu_send.at[n, 0], mu_recv.at[n, 0], to_near),
            remote(mu.at[n, OWN], mu.at[n, FAR], mu_send.at[n, 1], mu_recv.at[n, 1], mu_far),
        ]
        for c in copies[::-1]:
            c.start()
        mu_copies.extend(copies)
        if n == ITERS:
            for dx in (2, 1, 3):
                c = remote(mu.at[n, OWN], muin.at[dx], dip_send.at[dx], dip_recv.at[dx], peer(0, dx))
                c.start()
                dip_copies.append(c)

        columns(moment, OWN)
        acc = induce_part(n, OWN, (zero, zero, zero))
        for c, side in zip(copies, (NEAR, FAR)):
            c.wait_recv()
            columns(mu[n, side], side)
            acc = induce_part(n, side, acc)
        return rows_of(acc)

    moment = alpha * (cfield + rows_of(first))
    for n in range(1, ITERS):
        moment = alpha * (cfield + induce(n, moment))
    ind[...] = induce(ITERS, moment)
    ind_copies = []
    for dx in (2, 1, 3):
        c = remote(ind, indin.at[dx], ind_send.at[dx], ind_recv.at[dx], peer(0, dx))
        c.start()
        ind_copies.append(c)

    def put_moment(k, value):
        for a in range(3):
            moment_ref[a, pl.ds(k, 1), :] = value[a : a + 1]

    put_moment(spot, moment)
    total = [rows[l] + (8.0 * fold[0][l]) * ind[...] for l in range(beads)]
    for c, dx in zip(dip_copies, (2, 1, 3)):
        c.wait_recv()
        put_moment(lax.rem(spot + 4 - dx, 4), muin[dx])
    for c, dx in zip(ind_copies, (2, 1, 3)):
        c.wait_recv()
        total = [total[l] + (8.0 * fold[4 - dx][l]) * indin[dx] for l in range(beads)]
    for l in range(beads):
        for a in range(3):
            total_ref[a, l : l + 1, :] = total[l][a : a + 1]
    for c in halo + cp_copies + fp_copies + mu_copies + dip_copies + ind_copies:
        c.wait_send()


def solution(mesh):
    spaces = mesh.shape["space"]

    def body(positions, charges, polar, molecule):
        beads, _, atoms = positions.shape
        f32 = jnp.float32
        vmem = pl.BlockSpec(memory_space=pltpu.VMEM)
        dma = pltpu.SemaphoreType.DMA
        rounds = ITERS + 1
        total, moment = pl.pallas_call(
            functools.partial(kernel, beads, atoms, spaces),
            out_shape=(
                jax.ShapeDtypeStruct((3, beads, atoms), f32),
                jax.ShapeDtypeStruct((3, CONTR, atoms), f32),
            ),
            in_specs=[pl.BlockSpec(memory_space=pltpu.HBM)] * 4,
            out_specs=(vmem, vmem),
            scratch_shapes=[
                pltpu.VMEM((3, beads, atoms), f32),
                pltpu.VMEM((atoms,), f32), pltpu.VMEM((atoms,), f32), pltpu.VMEM((atoms,), jnp.int32),
                dma((4,)),
                pltpu.SemaphoreType.REGULAR,
                pltpu.VMEM((3, 16, atoms), f32),
                pltpu.VMEM((3, atoms, 16), f32),
                pltpu.VMEM((beads, 3, 8, atoms), f32),
                pltpu.VMEM((4, 3, 3, atoms), f32),
                pltpu.VMEM((7, 3, 3, atoms), f32),
                pltpu.VMEM((4, 3, atoms), f32),
                pltpu.VMEM((3, 8, 3, atoms), f32),
                pltpu.VMEM((3, 8, atoms), f32),
                pltpu.VMEM((3, atoms, 8), f32),
                pltpu.VMEM((3, 4, atoms, atoms), f32),
                pltpu.VMEM((rounds, 3, 3, atoms), f32),
                pltpu.VMEM((3, atoms, 8), f32),
                pltpu.VMEM((3, atoms), f32),
                pltpu.VMEM((4, 3, atoms), f32),
                pltpu.VMEM((4, 3, atoms), f32),
                dma((2,)), dma((2,)),
                dma((7,)), dma((7,)),
                dma((3, 8)), dma((3, 8)),
                dma((rounds, 2)), dma((rounds, 2)),
                dma((4,)), dma((4,)),
                dma((4,)), dma((4,)),
            ],
            compiler_params=pltpu.CompilerParams(
                collective_id=0, has_side_effects=True, vmem_limit_bytes=40 * 1024 * 1024
            ),
            name="polarize",
        )(
            *[
                pltpu.with_memory_space_constraint(x, pltpu.HBM)
                for x in (positions.transpose(1, 0, 2), charges, polar, molecule)
            ]
        )
        return total.transpose(1, 0, 2), moment.transpose(1, 0, 2)

    in_specs = (P("bead", None, "space"), P("space"), P("space"), P("space"))
    out_specs = (P("bead", None, "space"), P(None, None, "space"))
    return jax.shard_map(body, mesh=mesh, in_specs=in_specs, out_specs=out_specs, check_vma=False)
```
